32 devices in a mesh: dp: 4 (over y, x), tensor: 8 (over z, core).
Axes of the slice: x: 2, y: 2, z: 4, core: 2. Of those that a mesh axis runs over, the one named last changes fastest.
Arguments:
- tokens: bfloat16 [1024, 3072], P('dp', 'tensor'), may hold values from -6 to 6
- buckets: int32 [1024], P('dp'), may hold values from 0 to 999
- modulation: float32 [1000, 3, 3072], P(None, None, 'tensor'), may hold values from -3 to 3
- up_weight: bfloat16 [3072, 12288], P(None, 'tensor'), may hold values from -0.109375 to 0.109375
- down_weight: bfloat16 [3072, 12288], P(None, 'tensor'), may hold values from -0.0546875 to 0.0546875
- output_cotangent: bfloat16 [1024, 3072], P('dp', 'tensor'), may hold values from -6 to 6
Outputs:
- mixed: bfloat16 [1024, 3072], P('dp', 'tensor')
- token_input_gradient: bfloat16 [1024, 3072], P('dp', 'tensor')
- grad_up: float32 [3072, 12288], P('dp', 'tensor')
- grad_down: float32 [3072, 12288], P('dp', 'tensor')
The draws below stay inside these ranges and needn't reach their ends.
All inputs are finite; a program needn't handle non-finite values.
Results may differ from the reference program's by a relative error of at most 0.0062.
Values may be sent and summed in bfloat16 or wider, within the bound.
No kernel may reach another device: no remote copies, remote signals or barrier semaphores. Data moves between devices by JAX's collectives and lax.ppermute only.
A program may use at most 128 MiB of HBM per device.

```python
import jax
import jax.numpy as jnp
from jax import lax

D = 3072
FF = 12288
BUCKETS = 1000
TOKENS = 1024


def with_ends(values, own_key, least, top_value):
    longest = values.shape.index(max(values.shape))
    spots = []
    for shift in (0, 1):
        where = [jax.random.randint(jax.random.fold_in(own_key, axis), (), 0, length) for axis, length in enumerate(values.shape)]
        where[longest] = (where[longest] + shift) % values.shape[longest]
        spots.append(tuple(where))
    return values.at[spots[0]].set(least).at[spots[1]].set(top_value)


def shard_levels(key, dims, cuts, low, high):
    factor_of, own = 1.0, jax.random.fold_in(key, 6)
    for position, blocks in cuts:
        draws = jnp.exp(jax.random.uniform(jax.random.fold_in(own, position), (blocks,), jnp.float32, low / len(cuts), high / len(cuts)))
        factor_of = factor_of * jnp.repeat(draws, dims[position] // blocks).reshape([-1 if axis == position else 1 for axis in range(len(dims))])
    return factor_of


def gaussian(stream_key, dims, width, limit, cuts=(), kind=jnp.bfloat16):
    gain = shard_levels(stream_key, dims, cuts, -0.22, 0.18) if cuts else 1.0
    entries = jax.random.normal(stream_key, dims, jnp.float32) * width * gain
    return jnp.minimum(jnp.maximum(entries, -limit), limit).astype(kind)


def setup_inputs(seed: int = 0) -> dict:
    splits = jax.random.split(jax.random.key(seed), 7)
    return {
        "tokens": gaussian(splits[0], (TOKENS, D), 1.0, 6.0, ((0, 4), (1, 8))),
        "buckets": with_ends(jax.random.randint(splits[1], (TOKENS,), 0, BUCKETS), jax.random.fold_in(splits[1], 1), 0, BUCKETS - 1).astype(jnp.int32),
        "modulation": gaussian(splits[2], (BUCKETS, 3, D), 0.5, 3.0, ((2, 8),), jnp.float32),
        "up_weight": gaussian(splits[3], (D, FF), D ** -0.5, 0.109375, ((1, 8),)),
        "down_weight": gaussian(splits[4], (D, FF), FF ** -0.5, 0.0546875, ((1, 8),)),
        "output_cotangent": gaussian(splits[5], (TOKENS, D), 1.0, 6.0, ((0, 4), (1, 8))),
    }


def gelu_tanh(value):
    return jax.nn.gelu(value, approximate=True)

def reference(tokens, buckets, modulation, up_weight, down_weight, output_cotangent):
    model_width = tokens.shape[1]
    input_tokens = tokens.astype(jnp.float32)
    cond = jnp.take(modulation, buckets, axis=0)
    modulation_shift = cond[:, 0]
    modulation_scale = cond[:, 1]
    gate = cond[:, 2]
    row_mean = lax.optimization_barrier(jnp.sum(input_tokens, axis=1)) / model_width
    var = lax.optimization_barrier(jnp.sum(input_tokens * input_tokens, axis=1)) / model_width - row_mean * row_mean
    inverse_deviation = lax.rsqrt(var + 1e-06)
    normalized_input = (input_tokens - row_mean[:, None]) * inverse_deviation[:, None]
    hidden_input_rows = (normalized_input * (1.0 + modulation_scale) + modulation_shift).astype(jnp.bfloat16)
    pre = jnp.dot(hidden_input_rows, up_weight, preferred_element_type=jnp.float32)
    act = gelu_tanh(pre).astype(jnp.bfloat16)
    velocity = jnp.dot(act, down_weight.T, preferred_element_type=jnp.float32)
    mixed = (input_tokens + gate * velocity).astype(jnp.bfloat16)
    dvel = (output_cotangent.astype(jnp.float32) * gate).astype(jnp.bfloat16)
    dact = jnp.dot(dvel, down_weight, preferred_element_type=jnp.float32)
    pull = jax.vjp(gelu_tanh, pre)[1]
    dpre = pull(dact)[0].astype(jnp.bfloat16)
    grad_down = jnp.dot(dvel.T, act, preferred_element_type=jnp.float32)
    grad_up = jnp.dot(hidden_input_rows.T, dpre, preferred_element_type=jnp.float32)
    dh = jnp.dot(dpre, up_weight.T, preferred_element_type=jnp.float32)
    normalized_input_gradient = dh * (1.0 + modulation_scale)
    first_product = lax.optimization_barrier(jnp.sum(normalized_input_gradient, axis=1)) / model_width
    second_product = lax.optimization_barrier(jnp.sum(normalized_input_gradient * normalized_input, axis=1)) / model_width
    token_input_gradient = output_cotangent.astype(jnp.float32) + inverse_deviation[:, None] * (normalized_input_gradient - first_product[:, None] - normalized_input * second_product[:, None])
    return (mixed, token_input_gradient.astype(jnp.bfloat16), grad_up, grad_down)
```

```python
import functools
import math

import jax
import jax.numpy as jnp
from jax import lax
from jax.experimental import pallas as pl
from jax.experimental.pallas import tpu as pltpu
from jax.sharding import PartitionSpec as P

GELU_C = math.sqrt(2.0 / math.pi)
GELU_A = 0.044715
MIB = 1024 * 1024
F32 = jnp.float32
BF16 = jnp.bfloat16


def gelu_and_slope(v):
    square = v * v
    t = jnp.tanh(GELU_C * v * (1.0 + GELU_A * square))
    half = 0.5 * (1.0 + t)
    slope = half + (0.5 * GELU_C) * v * (1.0 - t * t) * (1.0 + (3.0 * GELU_A) * square)
    return v * half, slope


def column_tiles(length):
    tile = next((t for t in (256, 128) if length % t == 0), length)
    return [slice(start, start + tile) for start in range(0, length, tile)]


def call(kernel, name, operands, outs, scratch, flops):
    return pl.pallas_call(
        kernel,
        in_specs=[pl.BlockSpec(memory_space=pltpu.SMEM)]
        + [pl.BlockSpec(memory_space=pltpu.VMEM)] * (len(operands) - 1),
        out_specs=[pl.BlockSpec(memory_space=pltpu.VMEM)] * len(outs),
        out_shape=outs,
        scratch_shapes=scratch,
        compiler_params=pltpu.CompilerParams(vmem_limit_bytes=20 * MIB),
        cost_estimate=pl.CostEstimate(flops=flops, bytes_accessed=0, transcendentals=0),
        name=name,
    )(*operands)


def place(dest, pieces, spot):
    row = 0
    for piece in pieces:
        chips, rows, cols = piece[0].shape
        for k in range(chips):
            for side, ref in enumerate(piece):
                if len(piece) == 1:
                    dest[row : row + rows, :] = ref[k]
                else:
                    block = (spot[0] ^ k) * 2 + (spot[1] ^ side)
                    dest[row : row + rows, pl.ds(pl.multiple_of(block * cols, 128), cols)] = ref[k]
        row += rows


def split_refs(refs, sizes):
    pieces = []
    for size in sizes:
        pieces.append(refs[:size])
        refs = refs[size:]
    return pieces, refs


def dact_kernel(sizes, spot, *refs):
    pieces, (down, dact, dvel) = split_refs(refs, sizes)
    place(dvel, pieces, spot)
    for cols in column_tiles(down.shape[1]):
        dact[:, cols] = jnp.dot(dvel[...], down[:, cols], preferred_element_type=F32)


def dact_of(spot, pieces, down):
    width, hidden = down.shape
    rows = sum(piece[0].shape[1] for piece in pieces)
    return call(
        functools.partial(dact_kernel, [len(piece) for piece in pieces]),
        "dact",
        [spot, *[array for piece in pieces for array in piece], down],
        [jax.ShapeDtypeStruct((rows, hidden), F32)],
        [pltpu.VMEM((rows, width), BF16)],
        2 * rows * width * hidden,
    )[0]


def forward_tiles(h, dact, up, act, dpre):
    for cols in column_tiles(up.shape[1]):
        value, slope = gelu_and_slope(jnp.dot(h[...], up[:, cols], preferred_element_type=F32))
        act[:, cols] = value.astype(BF16)
        dpre[:, cols] = (dact[:, cols] * slope).astype(BF16)


def far_kernel(sizes, spot, *refs):
    pieces, (dact, up, act, dpre, h) = split_refs(refs, sizes)
    place(h, pieces, spot)
    forward_tiles(h, dact, up, act, dpre)


def far_chunk(spot, pieces, dact, up):
    width, hidden = up.shape
    rows = dact.shape[0]
    return call(
        functools.partial(far_kernel, [len(piece) for piece in pieces]),
        "far_tokens",
        [spot, *[array for piece in pieces for array in piece], dact, up],
        [jax.ShapeDtypeStruct((rows, hidden), BF16)] * 2,
        [pltpu.VMEM((rows, width), BF16)],
        2 * rows * width * hidden,
    )


def own_kernel(size, spot, *refs):
    piece, (dact, up, down, act, dpre, *parts, h, block) = split_refs(refs, [size])
    place(h, piece, spot)
    forward_tiles(h, dact, up, act, dpre)
    over = (((1,), (1,)), ((), ()))
    _, chips, _, cols = parts[0].shape
    wide = cols * len(parts)
    for q, (left, weight) in enumerate(((dpre, up), (act, down))):
        for k in range(chips):
            first = 0 if chips == 1 else pl.multiple_of((spot[0] ^ k) * wide, 128)
            block[...] = lax.dot_general(
                left[...], weight[pl.ds(first, wide), :], over, preferred_element_type=F32
            ).astype(BF16)
            for side, part in enumerate(parts):
                if len(parts) == 1:
                    part[q, k] = block[...]
                else:
                    part[q, k] = block[:, pl.ds(pl.multiple_of((spot[1] ^ side) * cols, 128), cols)]


def own_chunk(spot, piece, dact, up, down):
    width, hidden = up.shape
    chips, rows, cols = piece[0].shape
    return call(
        functools.partial(own_kernel, len(piece)),
        "own_tokens",
        [spot, *piece, dact, up, down],
        [jax.ShapeDtypeStruct((rows, hidden), BF16)] * 2
        + [jax.ShapeDtypeStruct((2, chips, rows, cols), BF16)] * len(piece),
        [pltpu.VMEM((rows, width), BF16), pltpu.VMEM((rows, cols * len(piece)), BF16)],
        6 * rows * width * hidden,
    )


def grad_kernel(sizes, groups, spot, *refs):
    both, refs = split_refs(refs, sizes * 2)
    acts, dpres = refs[:groups], refs[groups : 2 * groups]
    grad_up, grad_down, left, out, sems = refs[2 * groups :]
    over = (((0,), (0,)), ((), ()))
    copies = [None, None]
    turn = 0
    for grad, pieces, rights in ((grad_down, both[len(sizes) :], acts), (grad_up, both[: len(sizes)], dpres)):
        row = 0
        for piece in pieces:
            _, rows, cols = piece[0].shape
            for side, ref in enumerate(piece):
                if len(piece) == 1:
                    left[row : row + rows, :] = ref[0]
                else:
                    start = pl.multiple_of((spot[1] ^ side) * cols, 128)
                    left[row : row + rows, pl.ds(start, cols)] = ref[spot[2]]
            row += rows
        for cols in column_tiles(grad.shape[1]):
            row, total = 0, None
            for right in rights:
                rows = right.shape[0]
                part = lax.dot_general(left[row : row + rows], right[:, cols], over, preferred_element_type=F32)
                total = part if total is None else total + part
                row += rows
            slot = turn % 2
            if copies[slot] is not None:
                copies[slot].wait()
            out[slot] = total
            copies[slot] = pltpu.make_async_copy(out.at[slot], grad.at[:, cols], sems.at[slot])
            copies[slot].start()
            turn += 1
    for copy in copies:
        if copy is not None:
            copy.wait()


def weight_grads(spot, h_pieces, d_pieces, acts, dpres, height):
    hidden = acts[0].shape[1]
    tokens = sum(act.shape[0] for act in acts)
    tile = column_tiles(hidden)[0].stop
    operands = [spot, *[array for piece in h_pieces + d_pieces for array in piece], *acts, *dpres]
    return pl.pallas_call(
        functools.partial(grad_kernel, [len(piece) for piece in h_pieces], len(acts)),
        in_specs=[pl.BlockSpec(memory_space=pltpu.SMEM)]
        + [pl.BlockSpec(memory_space=pltpu.VMEM)] * (len(operands) - 1),
        out_specs=[pl.BlockSpec(memory_space=pl.ANY)] * 2,
        out_shape=[jax.ShapeDtypeStruct((height, hidden), F32)] * 2,
        scratch_shapes=[
            pltpu.VMEM((tokens, height), BF16),
            pltpu.VMEM((2, height, tile), F32),
            pltpu.SemaphoreType.DMA((2,)),
        ],
        compiler_params=pltpu.CompilerParams(vmem_limit_bytes=20 * MIB),
        cost_estimate=pl.CostEstimate(
            flops=4 * tokens * height * hidden, bytes_accessed=8 * height * hidden, transcendentals=0
        ),
        name="weight_grads",
    )(*operands)


def swap(value, axis, bits):
    size = lax.axis_size(axis)
    return lax.ppermute(value, axis, [(i, i ^ bits) for i in range(size)])


def chip_sum(value, chips):
    value = value + swap(value, "tensor", 1)
    parts = [swap(value, "tensor", 2 * k) for k in range(1, chips)]
    return sum(parts, value)


def spread(value, chips):
    return jnp.stack([value] + [swap(value, "tensor", 2 * k) for k in range(1, chips)])


def on_device(tokens, buckets, modulation, up_weight, down_weight, output_cotangent):
    rows, cols = tokens.shape
    chips = lax.axis_size("tensor") // 2
    groups = lax.axis_size("dp")
    width = cols * chips * 2
    blocked = cols % 128 == 0 and chips == groups
    place_in_tensor, group = lax.axis_index("tensor"), lax.axis_index("dp")
    chip, core = place_in_tensor // 2, place_in_tensor % 2
    spot = jnp.stack([chip, core, chip ^ group]).astype(jnp.int32)
    order = chip ^ jnp.arange(chips)

    def with_sibling(blocks):
        other = swap(blocks, "tensor", 1)
        if blocked:
            return blocks, other
        pair = jnp.stack([jnp.where(core == 0, blocks, other), jnp.where(core == 0, other, blocks)], axis=1)
        return (jnp.take(pair, order, axis=0).transpose(2, 0, 1, 3).reshape(1, blocks.shape[1], width),)

    x = tokens.astype(F32)
    cot = output_cotangent.astype(F32)
    cond = modulation.at[buckets].get(mode="promise_in_bounds")
    shift, scale, gate = cond[:, 0], cond[:, 1], cond[:, 2]
    dvel = (cot * gate).astype(BF16)
    sums = chip_sum(jnp.stack([jnp.sum(x, axis=1), jnp.sum(x * x, axis=1)]), chips)
    mean = sums[0] / width
    rstd = lax.rsqrt(sums[1] / width - mean * mean + 1e-06)[:, None]
    xhat = (x - mean[:, None]) * rstd
    h = (xhat * (1.0 + scale) + shift).astype(BF16)

    def gather(value):
        blocks = spread(value, chips)
        if groups != 4:
            return [[with_sibling(blocks)]] + [[with_sibling(swap(blocks, "dp", m))] for m in range(1, groups)]
        half = rows // 2
        left, right = swap(blocks, "dp", 1), swap(blocks, "dp", 2)
        corner = swap(left[:, :half], "dp", 2), swap(right[:, half:], "dp", 1)
        return [
            [with_sibling(blocks)],
            [with_sibling(left), with_sibling(right)],
            [with_sibling(piece) for piece in corner],
        ]

    d_groups, h_groups = gather(dvel), gather(h)
    acts, dpres = [], []
    for number, (h_pieces, d_pieces) in enumerate(zip(h_groups, d_groups)):
        dact = dact_of(spot, d_pieces, down_weight)
        if number == 0:
            act, dpre, *parts = own_chunk(spot, h_pieces[0], dact, up_weight, down_weight)
        else:
            act, dpre = far_chunk(spot, h_pieces, dact, up_weight)
        acts.append(act)
        dpres.append(dpre)

    if blocked:
        keep, give = parts
    else:
        pair = jnp.take(parts[0].reshape(2, rows, chips, 2, cols).transpose(0, 2, 3, 1, 4), order, axis=1)
        keep = jnp.where(core == 0, pair[:, :, 0], pair[:, :, 1])
        give = jnp.where(core == 0, pair[:, :, 1], pair[:, :, 0])
    mine = keep.astype(F32) + swap(give, "tensor", 1).astype(F32)
    sent = mine.astype(BF16)
    dh, velocity = [
        sum([swap(sent[q, k], "tensor", 2 * k).astype(F32) for k in range(1, chips)], mine[q, 0]) for q in (0, 1)
    ]
    mixed = (x + gate * velocity).astype(BF16)
    dxhat = dh * (1.0 + scale)
    sums = chip_sum(jnp.stack([jnp.sum(dxhat, axis=1), jnp.sum(dxhat * xhat, axis=1)]), chips) / width
    token_grad = cot + rstd * (dxhat - sums[0][:, None] - xhat * sums[1][:, None])

    height = width // groups
    h_pieces, d_pieces = [piece for g in h_groups for piece in g], [piece for g in d_groups for piece in g]
    if not blocked:
        mine_of = lambda piece: (lax.dynamic_slice_in_dim(piece[0], group * height, height, axis=2),)
        h_pieces, d_pieces = [mine_of(piece) for piece in h_pieces], [mine_of(piece) for piece in d_pieces]
    grad_up, grad_down = weight_grads(spot, h_pieces, d_pieces, acts, dpres, height)
    return mixed, token_grad.astype(BF16), grad_up, grad_down


def solution(mesh):
    rows, cols = P("dp", "tensor"), P(None, "tensor")
    return jax.shard_map(
        on_device,
        mesh=mesh,
        in_specs=(rows, P("dp"), P(None, None, "tensor"), cols, cols, rows),
        out_specs=(rows,) * 4,
        check_vma=False,
    )
```

```python
import functools
import math

import jax
import jax.numpy as jnp
from jax import lax
from jax.experimental import pallas as pl
from jax.experimental.pallas import tpu as pltpu
from jax.sharding import PartitionSpec as P

GELU_C = math.sqrt(2.0 / math.pi)
GELU_A = 0.044715
MIB = 1024 * 1024
F32 = jnp.float32
BF16 = jnp.bfloat16


def gelu_and_slope(v):
    square = v * v
    t = jnp.tanh(GELU_C * v * (1.0 + GELU_A * square))
    half = 0.5 * (1.0 + t)
    slope = half + (0.5 * GELU_C) * v * (1.0 - t * t) * (1.0 + (3.0 * GELU_A) * square)
    return v * half, slope


def column_tiles(length):
    tile = next((t for t in (256, 128) if length % t == 0), length)
    return [slice(start, start + tile) for start in range(0, length, tile)]


def call(kernel, name, operands, outs, scratch, flops):
    return pl.pallas_call(
        kernel,
        in_specs=[pl.BlockSpec(memory_space=pltpu.SMEM)]
        + [pl.BlockSpec(memory_space=pltpu.VMEM)] * (len(operands) - 1),
        out_specs=[pl.BlockSpec(memory_space=pltpu.VMEM)] * len(outs),
        out_shape=outs,
        scratch_shapes=scratch,
        compiler_params=pltpu.CompilerParams(vmem_limit_bytes=12 * MIB),
        cost_estimate=pl.CostEstimate(flops=8 * flops, bytes_accessed=0, transcendentals=0),
        name=name,
    )(*operands)


class Piece:
    def __init__(self, sides, bases=(0, 0)):
        self.sides = sides
        self.bases = bases

    def arrays(self):
        return [array for side in self.sides for _, array in side]

    def rows(self):
        return self.sides[0][0][1].shape[2]

    def bind(self, refs):
        refs = list(refs)
        return Piece([[(offset, refs.pop(0)) for offset, _ in side] for side in self.sides], self.bases)


def bind_all(pieces, refs):
    bound = []
    for piece in pieces:
        count = len(piece.arrays())
        bound.append(piece.bind(refs[:count]))
        refs = refs[count:]
    return bound, refs


def place(dest, row, piece, which, spot):
    rows = piece.rows()
    for side, (entries, base) in enumerate(zip(piece.sides, piece.bases)):
        for offset, ref in entries:
            cols = ref.shape[3]
            if len(piece.sides) == 1:
                dest[row : row + rows, :] = ref[base, which]
            else:
                block = (spot[0] ^ offset) * 2 + (spot[1] ^ side)
                dest[row : row + rows, pl.ds(pl.multiple_of(block * cols, 128), cols)] = ref[base, which]


def hidden_tiles(h, dvel, up, down, act, dpre):
    for cols in column_tiles(up.shape[1]):
        value, slope = gelu_and_slope(jnp.dot(h[...], up[:, cols], preferred_element_type=F32))
        act[:, cols] = value.astype(BF16)
        dact = jnp.dot(dvel[...], down[:, cols], preferred_element_type=F32)
        dpre[:, cols] = (dact * slope).astype(BF16)


def bring_kernel(spot, up, down, out):
    for j in range(spot.shape[0]):
        out[j] = spot[j]


def bring(spot, up, down):
    return pl.pallas_call(
        bring_kernel,
        in_specs=[pl.BlockSpec(memory_space=pltpu.SMEM)] + [pl.BlockSpec(memory_space=pltpu.VMEM)] * 2,
        out_specs=pl.BlockSpec(memory_space=pltpu.SMEM),
        out_shape=jax.ShapeDtypeStruct(spot.shape, spot.dtype),
        compiler_params=pltpu.CompilerParams(vmem_limit_bytes=MIB),
        name="bring_weights",
    )(spot, up, down)


def tokens_kernel(pieces, spot, *refs):
    pieces, (up, down, dpre, act, h_cols, d_cols, h, dvel) = bind_all(pieces, refs)
    row = 0
    for piece in pieces:
        place(h, row, piece, 0, spot)
        place(dvel, row, piece, 1, spot)
        row += piece.rows()
    height = h_cols.shape[1]
    mine = pl.ds(pl.multiple_of(spot[2] * height, 128), height)
    h_cols[...] = h[:, mine]
    d_cols[...] = dvel[:, mine]
    hidden_tiles(h, dvel, up, down, act, dpre)


def chunk_products(spot, pieces, up, down, height):
    width, hidden = up.shape
    rows = sum(piece.rows() for piece in pieces)
    return call(
        functools.partial(tokens_kernel, pieces),
        "chunk_products",
        [spot, *[array for piece in pieces for array in piece.arrays()], up, down],
        [jax.ShapeDtypeStruct((rows, hidden), BF16)] * 2 + [jax.ShapeDtypeStruct((rows, height), BF16)] * 2,
        [pltpu.VMEM((rows, width), BF16)] * 2,
        4 * rows * width * hidden,
    )


def back_kernel(left_spot, left, weight, *parts):
    *parts, block = parts
    chips, _, cols = parts[0].shape
    wide = cols * len(parts)
    for k in range(chips):
        first = 0 if chips == 1 else pl.multiple_of((left_spot[0] ^ k) * wide, 128)
        block[...] = lax.dot_general(
            left[...], weight[pl.ds(first, wide), :], (((1,), (1,)), ((), ())), preferred_element_type=F32
        ).astype(BF16)
        for side, part in enumerate(parts):
            if len(parts) == 1:
                part[k] = block[...]
            else:
                part[k] = block[:, pl.ds(pl.multiple_of((left_spot[1] ^ side) * cols, 128), cols)]


def back(spot, left, weight, chips, sides, name):
    rows, hidden = left.shape
    width = weight.shape[0]
    if sides == 1:
        chips = 1
    cols = width // (chips * sides)
    return call(
        back_kernel,
        name,
        [spot, left, weight],
        [jax.ShapeDtypeStruct((chips, rows, cols), BF16)] * sides,
        [pltpu.VMEM((rows, cols * sides), BF16)],
        2 * rows * width * hidden,
    )


def grad_kernel(chunks, *refs):
    sources, (grad_up, grad_down, left, right, out, sems) = refs[: 4 * chunks], refs[4 * chunks :]
    copies = [None, None]
    turn = 0
    for grad, first in ((grad_down, 1), (grad_up, 0)):
        row = 0
        for j in range(chunks):
            some = slice(row, row + sources[4 * j].shape[0])
            right[some, :] = sources[4 * j + first][...]
            left[some, :] = sources[4 * j + 2 + first][...]
            row = some.stop
        tile = out.shape[1]
        for start in range(0, grad.shape[0], tile):
            slot = turn % 2
            if copies[slot] is not None:
                copies[slot].wait()
            some = slice(start, start + tile)
            out[slot] = lax.dot_general(
                left[:, some], right[...], (((0,), (0,)), ((), ())), preferred_element_type=F32
            )
            copies[slot] = pltpu.make_async_copy(out.at[slot], grad.at[some], sems.at[slot])
            copies[slot].start()
            turn += 1
    for copy in copies:
        if copy is not None:
            copy.wait()


def weight_grads(chunks):
    tokens = sum(chunk[0].shape[0] for chunk in chunks)
    hidden, height = chunks[0][0].shape[1], chunks[0][2].shape[1]
    tile = next((t for t in (384, 256, 128) if height % t == 0), height)
    operands = [array for chunk in chunks for array in chunk]
    return pl.pallas_call(
        functools.partial(grad_kernel, len(chunks)),
        in_specs=[pl.BlockSpec(memory_space=pltpu.VMEM)] * len(operands),
        out_specs=[pl.BlockSpec(memory_space=pl.ANY)] * 2,
        out_shape=[jax.ShapeDtypeStruct((height, hidden), F32)] * 2,
        scratch_shapes=[
            pltpu.VMEM((tokens, height), BF16),
            pltpu.VMEM((tokens, hidden), BF16),
            pltpu.VMEM((2, tile, hidden), F32),
            pltpu.SemaphoreType.DMA((2,)),
        ],
        compiler_params=pltpu.CompilerParams(vmem_limit_bytes=12 * MIB),
        cost_estimate=pl.CostEstimate(flops=32 * tokens * height * hidden, bytes_accessed=0, transcendentals=0),
        name="weight_grads",
    )(*operands)


def swap(value, axis, bits):
    size = lax.axis_size(axis)
    return lax.ppermute(value, axis, [(i, i ^ bits) for i in range(size)])


def chip_sum(value, chips):
    value = value + swap(value, "tensor", 1)
    parts = [swap(value, "tensor", 2 * k) for k in range(1, chips)]
    return sum(parts, value)


def together(*values):
    return lax.optimization_barrier(values)


def spread(value, chips):
    offsets, blocks = [0], value[None]
    bit = chips // 2
    while bit > 1:
        offsets = offsets + [k ^ bit for k in offsets]
        blocks = jnp.concatenate([blocks, swap(blocks, "tensor", 2 * bit)])
        bit //= 2
    return (blocks, swap(blocks, "tensor", 2)), (offsets, [k ^ 1 for k in offsets])


def sum_over_chips(blocks):
    bit = 1
    while blocks.shape[1] > 1:
        sent = swap(blocks[:, 1::2].astype(BF16), "tensor", 2 * bit)
        blocks = blocks[:, 0::2] + sent.astype(F32)
        bit *= 2
    return blocks[:, 0]


def on_device(tokens, buckets, modulation, up_weight, down_weight, output_cotangent):
    rows, cols = tokens.shape
    chips = lax.axis_size("tensor") // 2
    groups = lax.axis_size("dp")
    width = cols * chips * 2
    height = width // groups
    blocked = cols % 128 == 0 and chips == groups
    place_in_tensor, group = lax.axis_index("tensor"), lax.axis_index("dp")
    chip, core = place_in_tensor // 2, place_in_tensor % 2
    spot = jnp.stack([chip, core, group]).astype(jnp.int32)
    order = chip ^ jnp.arange(chips)

    def with_sibling(arrays):
        other = [swap(array, "tensor", 1) for array in arrays]
        if blocked:
            blocks = lambda side: [
                (k, array[j : j + 1]) for ks, array in zip(offsets, side) for j, k in enumerate(ks)
            ]
            return Piece([blocks(arrays), blocks(other)])
        both = [jnp.concatenate(side) for side in (arrays, other)]
        pair = jnp.stack([jnp.where(core == 0, *both), jnp.where(core == 0, *both[::-1])], axis=1)
        pair = jnp.take(pair, jnp.argsort(jnp.array(sum(offsets, [])) ^ chip), axis=0)
        return Piece([[(0, pair.transpose(2, 3, 0, 1, 4).reshape(1, 2, rows, width))]])

    x = tokens.astype(F32)
    cot = output_cotangent.astype(F32)
    cond = modulation.at[buckets].get(mode="promise_in_bounds")
    shift, scale, gate = cond[:, 0], cond[:, 1], cond[:, 2]
    dvel = (cot * gate).astype(BF16)
    sums = chip_sum(jnp.stack([jnp.sum(x, axis=1), jnp.sum(x * x, axis=1)]), chips)
    mean = sums[0] / width
    rstd = lax.rsqrt(sums[1] / width - mean * mean + 1e-06)[:, None]
    xhat = (x - mean[:, None]) * rstd
    h = (xhat * (1.0 + scale) + shift).astype(BF16)

    spot = bring(spot, up_weight, down_weight)
    value = jnp.stack([h, dvel])
    if chips == 4 and groups == 4 and blocked:
        along_z = lambda array, k: swap(array, "tensor", 2 * k)
        sibling = lambda array: swap(array, "tensor", 1)
        piece = lambda mine, others, *bases: Piece([list(enumerate(mine)), list(enumerate(others))], bases)

        near0 = value[None]
        near1, near2, left0, right0, near0_s, spot = together(
            along_z(near0, 1), along_z(near0, 2), swap(near0, "dp", 1), swap(near0, "dp", 2), sibling(near0), spot
        )
        near3, left1, right1, near1_s, near2_s = together(
            along_z(near2, 1), swap(near1, "dp", 1), swap(near1, "dp", 2), sibling(near1), sibling(near2)
        )
        near = piece((near0, near1, near2, near3), (near0_s, near1_s, near2_s, sibling(near3)), 0, 0)
        own = chunk_products(spot, [near], up_weight, down_weight, height)
        keep_dh, give_dh = back(spot, own[0], up_weight, chips, 2, "dh_share")
        keep_dh, give_dh, own, left2, right2 = together(
            keep_dh, give_dh, own, swap(near2, "dp", 1), swap(near2, "dp", 2)
        )
        far0, far1, far2 = [jnp.concatenate(p) for p in ((left0, right0), (left1, right1), (left2, right2))]
        keep_vel, give_vel = back(spot, own[1], down_weight, chips, 2, "velocity_share")
        keep_vel, give_vel, given_dh, left3, right3, *others = together(
            keep_vel,
            give_vel,
            sibling(give_dh),
            swap(near3, "dp", 1),
            swap(near3, "dp", 2),
            *map(sibling, (far0, far1, far2)),
        )
        given_vel, far3_s, keep_dh, corner02, corner13 = together(
            sibling(give_vel),
            sibling(jnp.concatenate((left3, right3))),
            keep_dh,
            jnp.concatenate((left0, left2)),
            jnp.concatenate((right1, right3)),
        )
        others.append(far3_s)
        dh = keep_dh.astype(F32) + given_dh.astype(F32)
        dh_parts = [along_z(dh[k].astype(BF16), k) for k in (1, 2, 3)]
        left = piece((left0, left1, left2, left3), others, 0, 0)
        right = piece((right0, right1, right2, right3), others, 0, 1)
        distant = chunk_products(spot, [left, right], up_weight, down_weight, height)
        distant, keep_vel, corner02, corner13, *dh_parts = together(
            distant, keep_vel, swap(corner02, "dp", 2), swap(corner13, "dp", 1), *dh_parts
        )
        dh = sum([part.astype(F32) for part in dh_parts], dh[0])
        dxhat = dh * (1.0 + scale)
        sums = jnp.stack([jnp.sum(dxhat, axis=1), jnp.sum(dxhat * xhat, axis=1)])
        dxhat, gate, sums, sums_s, corner02_s, corner13_s = together(
            dxhat, gate, sums, sibling(sums), sibling(corner02), sibling(corner13)
        )
        velocity = keep_vel.astype(F32) + given_vel.astype(F32)
        vel_parts = [along_z(velocity[k].astype(BF16), k) for k in (1, 2, 3)]
        sums = sums + sums_s
        sums = sums + along_z(sums, 1)
        corner = Piece(
            [
                [(0, corner02[:1]), (1, corner13[:1]), (2, corner02[1:]), (3, corner13[1:])],
                [(0, corner02_s[:1]), (1, corner13_s[:1]), (2, corner02_s[1:]), (3, corner13_s[1:])],
            ]
        )
        last = chunk_products(spot, [corner], up_weight, down_weight, height)
        last, sums = together(last, sums)
        sums = (sums + along_z(sums, 2)) / width
        velocity = sum([part.astype(F32) for part in vel_parts], velocity[0])
        chunks = [own, distant, last]
    else:
        arrays, offsets = spread(value, chips)
        near = with_sibling(arrays)
        chunks = [chunk_products(spot, [near], up_weight, down_weight, height)]
        shares = [
            back(spot, chunks[0][j], weight, chips, len(near.sides), name)
            for j, weight, name in ((0, up_weight, "dh_share"), (1, down_weight, "velocity_share"))
        ]
        if blocked:
            keep, give = map(jnp.stack, zip(*shares))
        else:
            pair = jnp.concatenate([share[0] for share in shares])
            pair = jnp.take(pair.reshape(2, rows, chips, 2, cols).transpose(0, 2, 3, 1, 4), order, axis=1)
            keep = jnp.where(core == 0, pair[:, :, 0], pair[:, :, 1])
            give = jnp.where(core == 0, pair[:, :, 1], pair[:, :, 0])
        dh, velocity = sum_over_chips(keep.astype(F32) + swap(give, "tensor", 1).astype(F32))
        for m in range(1, groups):
            far = with_sibling([swap(array, "dp", m) for array in arrays])
            chunks.append(chunk_products(spot, [far], up_weight, down_weight, height))
        dxhat = dh * (1.0 + scale)
        sums = chip_sum(jnp.stack([jnp.sum(dxhat, axis=1), jnp.sum(dxhat * xhat, axis=1)]), chips) / width
    mixed = (x + gate * velocity).astype(BF16)
    token_grad = cot + rstd * (dxhat - sums[0][:, None] - xhat * sums[1][:, None])

    grad_up, grad_down = weight_grads(chunks)
    return mixed, token_grad.astype(BF16), grad_up, grad_down


def solution(mesh):
    rows, cols = P("dp", "tensor"), P(None, "tensor")
    return jax.shard_map(
        on_device,
        mesh=mesh,
        in_specs=(rows, P("dp"), P(None, None, "tensor"), cols, cols, rows),
        out_specs=(rows,) * 4,
        check_vma=False,
    )
```

```python
import functools
import math

import jax
import jax.numpy as jnp
from jax import lax
from jax.experimental import pallas as pl
from jax.experimental.pallas import tpu as pltpu
from jax.sharding import PartitionSpec as P

GELU_C = math.sqrt(2.0 / math.pi)
GELU_A = 0.044715
MIB = 1024 * 1024
F32 = jnp.float32
BF16 = jnp.bfloat16


def gelu_and_slope(v):
    square = v * v
    t = jnp.tanh(GELU_C * v * (1.0 + GELU_A * square))
    half = 0.5 * (1.0 + t)
    slope = half + (0.5 * GELU_C) * v * (1.0 - t * t) * (1.0 + (3.0 * GELU_A) * square)
    return v * half, slope


def each_column_tile(length, body, loop):
    tile = next((t for t in (256, 128) if length % t == 0), length)
    if not loop:
        for start in range(0, length, tile):
            body(slice(start, start + tile))
        return

    @pl.loop(0, length // tile)
    def _(i):
        body(pl.ds(pl.multiple_of(i * tile, 128), tile))


def call(kernel, name, operands, outs, scratch, flops, weight=8):
    return pl.pallas_call(
        kernel,
        in_specs=[pl.BlockSpec(memory_space=pltpu.SMEM)]
        + [pl.BlockSpec(memory_space=pltpu.VMEM)] * (len(operands) - 1),
        out_specs=[pl.BlockSpec(memory_space=pltpu.VMEM)] * len(outs),
        out_shape=outs,
        scratch_shapes=scratch,
        compiler_params=pltpu.CompilerParams(vmem_limit_bytes=12 * MIB),
        cost_estimate=pl.CostEstimate(flops=int(weight * flops), bytes_accessed=0, transcendentals=0),
        name=name,
    )(*operands)


class Piece:
    def __init__(self, sides):
        self.sides = sides

    def arrays(self):
        return [array for side in self.sides for _, _, array in side]

    def rows(self):
        return self.sides[0][0][2].shape[2]

    def bind(self, refs):
        refs = list(refs)
        return Piece([[(offset, index, refs.pop(0)) for offset, index, _ in side] for side in self.sides])


def bind_all(pieces, refs):
    bound = []
    for piece in pieces:
        count = len(piece.arrays())
        bound.append(piece.bind(refs[:count]))
        refs = refs[count:]
    return bound, refs


def place(dest, row, piece, which, spot):
    rows = piece.rows()
    for side, entries in enumerate(piece.sides):
        for offset, base, ref in entries:
            cols = ref.shape[3]
            if len(piece.sides) == 1:
                dest[row : row + rows, :] = ref[base, which]
            else:
                block = (spot[0] ^ offset) * 2 + (spot[1] ^ side)
                dest[row : row + rows, pl.ds(pl.multiple_of(block * cols, 128), cols)] = ref[base, which]


def hidden_tiles(h, dvel, up, down, act, dpre):
    def products(cols):
        value, slope = gelu_and_slope(jnp.dot(h[...], up[:, cols], preferred_element_type=F32))
        act[:, cols] = value.astype(BF16)
        dact = jnp.dot(dvel[...], down[:, cols], preferred_element_type=F32)
        dpre[:, cols] = (dact * slope).astype(BF16)

    each_column_tile(up.shape[1], products, loop=h.shape[0] > 256)


def bring_kernel(spot, up, down, out):
    for j in range(spot.shape[0]):
        out[j] = spot[j]


def bring(spot, up, down):
    return pl.pallas_call(
        bring_kernel,
        in_specs=[pl.BlockSpec(memory_space=pltpu.SMEM)] + [pl.BlockSpec(memory_space=pltpu.VMEM)] * 2,
        out_specs=pl.BlockSpec(memory_space=pltpu.SMEM),
        out_shape=jax.ShapeDtypeStruct(spot.shape, spot.dtype),
        compiler_params=pltpu.CompilerParams(vmem_limit_bytes=MIB),
        name="bring_weights",
    )(spot, up, down)


def tokens_kernel(pieces, spot, *refs):
    pieces, (up, down, dpre, act, h_cols, d_cols, h, dvel) = bind_all(pieces, refs)
    row = 0
    for piece in pieces:
        place(h, row, piece, 0, spot)
        place(dvel, row, piece, 1, spot)
        row += piece.rows()
    height = h_cols.shape[1]
    mine = pl.ds(pl.multiple_of(spot[2] * height, 128), height)
    h_cols[...] = h[:, mine]
    d_cols[...] = dvel[:, mine]
    hidden_tiles(h, dvel, up, down, act, dpre)


def chunk_products(spot, pieces, up, down, height, weight=8):
    width, hidden = up.shape
    rows = sum(piece.rows() for piece in pieces)
    return call(
        functools.partial(tokens_kernel, pieces),
        "chunk_products",
        [spot, *[array for piece in pieces for array in piece.arrays()], up, down],
        [jax.ShapeDtypeStruct((rows, hidden), BF16)] * 2 + [jax.ShapeDtypeStruct((rows, height), BF16)] * 2,
        [pltpu.VMEM((rows, width), BF16)] * 2,
        4 * rows * width * hidden,
        weight,
    )


def back_kernel(left_spot, left, weight, *parts):
    *parts, block = parts
    chips, _, cols = parts[0].shape
    wide = cols * len(parts)
    for k in range(chips):
        first = 0 if chips == 1 else pl.multiple_of((left_spot[0] ^ k) * wide, 128)
        block[...] = lax.dot_general(
            left[...], weight[pl.ds(first, wide), :], (((1,), (1,)), ((), ())), preferred_element_type=F32
        ).astype(BF16)
        for side, part in enumerate(parts):
            if len(parts) == 1:
                part[k] = block[...]
            else:
                part[k] = block[:, pl.ds(pl.multiple_of((left_spot[1] ^ side) * cols, 128), cols)]


def back(spot, left, weight, chips, sides, name):
    rows, hidden = left.shape
    width = weight.shape[0]
    if sides == 1:
        chips = 1
    cols = width // (chips * sides)
    return call(
        back_kernel,
        name,
        [spot, left, weight],
        [jax.ShapeDtypeStruct((chips, rows, cols), BF16)] * sides,
        [pltpu.VMEM((rows, cols * sides), BF16)],
        2 * rows * width * hidden,
    )


def grad_kernel(chunks, *refs):
    sources, (grad_up, grad_down, left, right, out, sems) = refs[: 4 * chunks], refs[4 * chunks :]
    copies = [None, None]
    turn = 0
    for grad, first in ((grad_down, 1), (grad_up, 0)):
        row = 0
        for j in range(chunks):
            some = slice(row, row + sources[4 * j].shape[0])
            right[some, :] = sources[4 * j + first][...]
            left[some, :] = sources[4 * j + 2 + first][...]
            row = some.stop
        tile = out.shape[1]
        for start in range(0, grad.shape[0], tile):
            slot = turn % 2
            if copies[slot] is not None:
                copies[slot].wait()
            some = slice(start, start + tile)

            out[slot] = lax.dot_general(
                left[:, some], right[...], (((0,), (0,)), ((), ())), preferred_element_type=F32
            )
            copies[slot] = pltpu.make_async_copy(out.at[slot], grad.at[some], sems.at[slot])
            copies[slot].start()
            turn += 1
    for copy in copies:
        if copy is not None:
            copy.wait()


def weight_grads(chunks):
    tokens = sum(chunk[0].shape[0] for chunk in chunks)
    hidden, height = chunks[0][0].shape[1], chunks[0][2].shape[1]
    tile = next((t for t in (384, 256, 128) if height % t == 0), height)
    operands = [array for chunk in chunks for array in chunk]
    return pl.pallas_call(
        functools.partial(grad_kernel, len(chunks)),
        in_specs=[pl.BlockSpec(memory_space=pltpu.VMEM)] * len(operands),
        out_specs=[pl.BlockSpec(memory_space=pl.ANY)] * 2,
        out_shape=[jax.ShapeDtypeStruct((height, hidden), F32)] * 2,
        scratch_shapes=[
            pltpu.VMEM((tokens, height), BF16),
            pltpu.VMEM((tokens, hidden), BF16),
            pltpu.VMEM((2, tile, hidden), F32),
            pltpu.SemaphoreType.DMA((2,)),
        ],
        compiler_params=pltpu.CompilerParams(vmem_limit_bytes=12 * MIB),
        cost_estimate=pl.CostEstimate(flops=32 * tokens * height * hidden, bytes_accessed=0, transcendentals=0),
        name="weight_grads",
    )(*operands)


def swap(value, axis, bits):
    size = lax.axis_size(axis)
    return lax.ppermute(value, axis, [(i, i ^ bits) for i in range(size)])


def chip_sum(value, chips):
    value = value + swap(value, "tensor", 1)
    parts = [swap(value, "tensor", 2 * k) for k in range(1, chips)]
    return sum(parts, value)


def together(*values):
    return lax.optimization_barrier(values)


def spread(value, chips):
    offsets, blocks = [0], value[None]
    bit = chips // 2
    while bit > 1:
        offsets = offsets + [k ^ bit for k in offsets]
        blocks = jnp.concatenate([blocks, swap(blocks, "tensor", 2 * bit)])
        bit //= 2
    return (blocks, swap(blocks, "tensor", 2)), (offsets, [k ^ 1 for k in offsets])


def sum_over_chips(blocks):
    bit = 1
    while blocks.shape[1] > 1:
        sent = swap(blocks[:, 1::2].astype(BF16), "tensor", 2 * bit)
        blocks = blocks[:, 0::2] + sent.astype(F32)
        bit *= 2
    return blocks[:, 0]


def on_device(tokens, buckets, modulation, up_weight, down_weight, output_cotangent):
    rows, cols = tokens.shape
    chips = lax.axis_size("tensor") // 2
    groups = lax.axis_size("dp")
    width = cols * chips * 2
    height = width // groups
    blocked = cols % 128 == 0 and chips == groups
    place_in_tensor, group = lax.axis_index("tensor"), lax.axis_index("dp")
    chip, core = place_in_tensor // 2, place_in_tensor % 2
    spot = jnp.stack([chip, core, group]).astype(jnp.int32)
    order = chip ^ jnp.arange(chips)

    def with_sibling(arrays):
        other = [swap(array, "tensor", 1) for array in arrays]
        if blocked:
            blocks = lambda side: [
                (k, j, array) for ks, array in zip(offsets, side) for j, k in enumerate(ks)
            ]
            return Piece([blocks(arrays), blocks(other)])
        both = [jnp.concatenate(side) for side in (arrays, other)]
        pair = jnp.stack([jnp.where(core == 0, *both), jnp.where(core == 0, *both[::-1])], axis=1)
        pair = jnp.take(pair, jnp.argsort(jnp.array(sum(offsets, [])) ^ chip), axis=0)
        return Piece([[(0, 0, pair.transpose(2, 3, 0, 1, 4).reshape(1, 2, rows, width))]])

    x = tokens.astype(F32)
    cot = output_cotangent.astype(F32)
    cond = modulation.at[buckets].get(mode="promise_in_bounds")
    shift, scale, gate = cond[:, 0], cond[:, 1], cond[:, 2]
    dvel = (cot * gate).astype(BF16)
    sums = chip_sum(jnp.stack([jnp.sum(x, axis=1), jnp.sum(x * x, axis=1)]), chips)
    mean = sums[0] / width
    rstd = lax.rsqrt(sums[1] / width - mean * mean + 1e-06)[:, None]
    xhat = (x - mean[:, None]) * rstd
    h = (xhat * (1.0 + scale) + shift).astype(BF16)

    spot = bring(spot, up_weight, down_weight)
    value = jnp.stack([h, dvel])
    if chips == 4 and groups == 4 and blocked:
        along_z = lambda array, k: swap(array, "tensor", 2 * k)
        sibling = lambda array: swap(array, "tensor", 1)
        piece = lambda *sides: Piece([[(k, *block) for k, block in enumerate(side)] for side in sides])

        near0 = value[None]
        near1, near2, left0, right0, near0_s, spot = together(
            along_z(near0, 1), along_z(near0, 2), swap(near0, "dp", 1), swap(near0, "dp", 2), sibling(near0), spot
        )
        near3, left1, right1, near1_s, near2_s = together(
            along_z(near2, 1), swap(near1, "dp", 1), swap(near1, "dp", 2), sibling(near1), sibling(near2)
        )
        near23 = jnp.concatenate((near2, near3))
        near = piece(
            ((0, near0), (0, near1), (0, near2), (0, near3)),
            ((0, near0_s), (0, near1_s), (0, near2_s), (0, sibling(near3))),
        )
        own = chunk_products(spot, [near], up_weight, down_weight, height)
        keep_dh, give_dh = back(spot, own[0], up_weight, chips, 2, "dh_share")
        given_dh = sibling(give_dh)
        keep_vel, give_vel = back(spot, own[1], down_weight, chips, 2, "velocity_share")
        far01 = jnp.concatenate((left0, right0, left1, right1))
        own, keep_dh, given_dh, keep_vel, give_vel, far01_s, left23, right23 = together(
            own, keep_dh, given_dh, keep_vel, give_vel, sibling(far01), swap(near23, "dp", 1), swap(near23, "dp", 2)
        )
        given_vel, far23_s = together(sibling(give_vel), sibling(jnp.concatenate((left23, right23))))
        dh = keep_dh.astype(F32) + given_dh.astype(F32)
        corner02, corner13 = jnp.concatenate((left0, left23[:1])), jnp.concatenate((right1, right23[1:]))
        shares = jnp.stack((dh, keep_vel.astype(F32) + given_vel.astype(F32)))
        corner02, corner13 = swap(corner02, "dp", 2), swap(corner13, "dp", 1)
        left = piece(
            ((0, left0), (0, left1), (0, left23), (1, left23)),
            ((0, far01_s), (2, far01_s), (0, far23_s), (1, far23_s)),
        )
        right = piece(
            ((0, right0), (0, right1), (0, right23), (1, right23)),
            ((1, far01_s), (3, far01_s), (2, far23_s), (3, far23_s)),
        )
        distant = chunk_products(spot, [left, right], up_weight, down_weight, height)
        distant, halves, corner02, corner13 = together(
            distant, along_z(shares[:, 1::2].astype(BF16), 1), corner02, corner13
        )
        shares = shares[:, ::2] + halves.astype(F32)
        sent_dh, sent_vel = shares[0, 1].astype(BF16), shares[1, 1].astype(BF16)
        got_dh = along_z(sent_dh, 2)
        corner02_s, corner13_s = sibling(corner02), sibling(corner13)
        corner = piece(
            ((0, corner02), (0, corner13), (1, corner02), (1, corner13)),
            ((0, corner02_s), (0, corner13_s), (1, corner02_s), (1, corner13_s)),
        )
        last = chunk_products(spot, [corner], up_weight, down_weight, height)
        last, got_dh, sent_vel = together(last, got_dh, sent_vel)
        dh = shares[0, 0] + got_dh.astype(F32)
        dxhat = dh * (1.0 + scale)
        sums = jnp.stack([jnp.sum(dxhat, axis=1), jnp.sum(dxhat * xhat, axis=1)])
        sums, gate = together(sums, gate)
        sums = sums + sibling(sums)
        sums = (sums + along_z(sums, 1) + along_z(sums, 2) + along_z(sums, 3)) / width
        velocity = shares[1, 0] + along_z(sent_vel, 2).astype(F32)
        chunks = [own, distant, last]
    else:
        arrays, offsets = spread(value, chips)
        near = with_sibling(arrays)
        chunks = [chunk_products(spot, [near], up_weight, down_weight, height)]
        shares = [
            back(spot, chunks[0][j], weight, chips, len(near.sides), name)
            for j, weight, name in ((0, up_weight, "dh_share"), (1, down_weight, "velocity_share"))
        ]
        if blocked:
            keep, give = map(jnp.stack, zip(*shares))
        else:
            pair = jnp.concatenate([share[0] for share in shares])
            pair = jnp.take(pair.reshape(2, rows, chips, 2, cols).transpose(0, 2, 3, 1, 4), order, axis=1)
            keep = jnp.where(core == 0, pair[:, :, 0], pair[:, :, 1])
            give = jnp.where(core == 0, pair[:, :, 1], pair[:, :, 0])
        dh, velocity = sum_over_chips(keep.astype(F32) + swap(give, "tensor", 1).astype(F32))
        for m in range(1, groups):
            far = with_sibling([swap(array, "dp", m) for array in arrays])
            chunks.append(chunk_products(spot, [far], up_weight, down_weight, height))
        dxhat = dh * (1.0 + scale)
        sums = chip_sum(jnp.stack([jnp.sum(dxhat, axis=1), jnp.sum(dxhat * xhat, axis=1)]), chips) / width
    mixed = (x + gate * velocity).astype(BF16)
    token_grad = cot + rstd * (dxhat - sums[0][:, None] - xhat * sums[1][:, None])

    grad_up, grad_down = weight_grads(chunks)
    return mixed, token_grad.astype(BF16), grad_up, grad_down


def solution(mesh):
    rows, cols = P("dp", "tensor"), P(None, "tensor")
    return jax.shard_map(
        on_device,
        mesh=mesh,
        in_specs=(rows, P("dp"), P(None, None, "tensor"), cols, cols, rows),
        out_specs=(rows,) * 4,
        check_vma=False,
    )
```

```python
import functools
import math

import jax
import jax.numpy as jnp
from jax import lax
from jax.experimental import pallas as pl
from jax.experimental.pallas import tpu as pltpu
from jax.sharding import PartitionSpec as P

GELU_C = math.sqrt(2.0 / math.pi)
GELU_A = 0.044715
MIB = 1024 * 1024
F32 = jnp.float32
BF16 = jnp.bfloat16


def gelu_and_slope(v):
    square = v * v
    t = jnp.tanh(GELU_C * v * (1.0 + GELU_A * square))
    half = 0.5 * (1.0 + t)
    slope = half + (0.5 * GELU_C) * v * (1.0 - t * t) * (1.0 + (3.0 * GELU_A) * square)
    return v * half, slope


def each_column_tile(length, body, loop):
    tile = next((t for t in ((512,) * loop + (256, 128)) if length % t == 0), length)
    if not loop:
        for start in range(0, length, tile):
            body(slice(start, start + tile))
        return

    @pl.loop(0, length // tile)
    def _(i):
        body(pl.ds(pl.multiple_of(i * tile, 128), tile))


def call(kernel, name, operands, outs, scratch, flops, weight=8):
    return pl.pallas_call(
        kernel,
        in_specs=[pl.BlockSpec(memory_space=pltpu.SMEM)]
        + [pl.BlockSpec(memory_space=pltpu.VMEM)] * (len(operands) - 1),
        out_specs=[pl.BlockSpec(memory_space=pltpu.VMEM)] * len(outs),
        out_shape=outs,
        scratch_shapes=scratch,
        compiler_params=pltpu.CompilerParams(vmem_limit_bytes=9 * MIB),
        cost_estimate=pl.CostEstimate(flops=int(weight * flops), bytes_accessed=0, transcendentals=0),
        name=name,
    )(*operands)


class Piece:
    def __init__(self, sides):
        self.sides = sides

    def arrays(self):
        return [array for side in self.sides for _, _, array in side]

    def rows(self):
        return self.sides[0][0][2].shape[2]

    def bind(self, refs):
        refs = list(refs)
        return Piece([[(offset, index, refs.pop(0)) for offset, index, _ in side] for side in self.sides])


def bind_all(pieces, refs):
    bound = []
    for piece in pieces:
        count = len(piece.arrays())
        bound.append(piece.bind(refs[:count]))
        refs = refs[count:]
    return bound, refs


def place(dest, row, piece, which, spot):
    rows = piece.rows()
    for side, entries in enumerate(piece.sides):
        for offset, base, ref in entries:
            cols = ref.shape[3]
            if len(piece.sides) == 1:
                dest[row : row + rows, :] = ref[base, which]
            else:
                block = (spot[0] ^ offset) * 2 + (spot[1] ^ side)
                dest[row : row + rows, pl.ds(pl.multiple_of(block * cols, 128), cols)] = ref[base, which]


def hidden_tiles(h, dvel, up, down, act, dpre):
    def products(cols):
        value, slope = gelu_and_slope(jnp.dot(h[...], up[:, cols], preferred_element_type=F32))
        act[:, cols] = value.astype(BF16)
        dact = jnp.dot(dvel[...], down[:, cols], preferred_element_type=F32)
        dpre[:, cols] = (dact * slope).astype(BF16)

    each_column_tile(up.shape[1], products, loop=h.shape[0] > 256)


def bring_kernel(spot, up, down, out):
    for j in range(spot.shape[0]):
        out[j] = spot[j]


def bring(spot, up, down):
    return pl.pallas_call(
        bring_kernel,
        in_specs=[pl.BlockSpec(memory_space=pltpu.SMEM)] + [pl.BlockSpec(memory_space=pltpu.VMEM)] * 2,
        out_specs=pl.BlockSpec(memory_space=pltpu.SMEM),
        out_shape=jax.ShapeDtypeStruct(spot.shape, spot.dtype),
        compiler_params=pltpu.CompilerParams(vmem_limit_bytes=MIB),
        name="bring_weights",
    )(spot, up, down)


def tokens_kernel(pieces, spot, *refs):
    pieces, (up, down, dpre, act, h_cols, d_cols, h, dvel) = bind_all(pieces, refs)
    row = 0
    for piece in pieces:
        place(h, row, piece, 0, spot)
        place(dvel, row, piece, 1, spot)
        row += piece.rows()
    height = h_cols.shape[1]
    mine = pl.ds(pl.multiple_of(spot[2] * height, 128), height)
    h_cols[...] = h[:, mine]
    d_cols[...] = dvel[:, mine]
    hidden_tiles(h, dvel, up, down, act, dpre)


def chunk_products(spot, pieces, up, down, height, weight=8):
    width, hidden = up.shape
    rows = sum(piece.rows() for piece in pieces)
    return call(
        functools.partial(tokens_kernel, pieces),
        "chunk_products",
        [spot, *[array for piece in pieces for array in piece.arrays()], up, down],
        [jax.ShapeDtypeStruct((rows, hidden), BF16)] * 2 + [jax.ShapeDtypeStruct((rows, height), BF16)] * 2,
        [pltpu.VMEM((rows, width), BF16)] * 2,
        4 * rows * width * hidden,
        weight,
    )


def back_kernel(left_spot, left, weight, *parts):
    *parts, block = parts
    chips, _, cols = parts[0].shape
    wide = cols * len(parts)
    for k in range(chips):
        first = 0 if chips == 1 else pl.multiple_of((left_spot[0] ^ k) * wide, 128)
        block[...] = lax.dot_general(
            left[...], weight[pl.ds(first, wide), :], (((1,), (1,)), ((), ())), preferred_element_type=F32
        ).astype(BF16)
        for side, part in enumerate(parts):
            if len(parts) == 1:
                part[k] = block[...]
            else:
                part[k] = block[:, pl.ds(pl.multiple_of((left_spot[1] ^ side) * cols, 128), cols)]


def back(spot, left, weight, chips, sides, name):
    rows, hidden = left.shape
    width = weight.shape[0]
    if sides == 1:
        chips = 1
    cols = width // (chips * sides)
    return call(
        back_kernel,
        name,
        [spot, left, weight],
        [jax.ShapeDtypeStruct((chips, rows, cols), BF16)] * sides,
        [pltpu.VMEM((rows, cols * sides), BF16)],
        2 * rows * width * hidden,
    )


def grad_kernel(chunks, *refs):
    sources, (grad_up, grad_down, left, right, out, sems) = refs[: 4 * chunks], refs[4 * chunks :]
    copies = [None, None]
    turn = 0
    for grad, first in ((grad_down, 1), (grad_up, 0)):
        row = 0
        for j in range(chunks):
            some = slice(row, row + sources[4 * j].shape[0])
            right[some, :] = sources[4 * j + first][...]
            left[some, :] = sources[4 * j + 2 + first][...]
            row = some.stop
        tile = out.shape[1]
        for start in range(0, grad.shape[0], tile):
            slot = turn % 2
            if copies[slot] is not None:
                copies[slot].wait()
            some = slice(start, start + tile)

            out[slot] = lax.dot_general(
                left[:, some], right[...], (((0,), (0,)), ((), ())), preferred_element_type=F32
            )
            copies[slot] = pltpu.make_async_copy(out.at[slot], grad.at[some], sems.at[slot])
            copies[slot].start()
            turn += 1
    for copy in copies:
        if copy is not None:
            copy.wait()


def weight_grads(chunks):
    tokens = sum(chunk[0].shape[0] for chunk in chunks)
    hidden, height = chunks[0][0].shape[1], chunks[0][2].shape[1]
    tile = next((t for t in (384, 256, 128) if height % t == 0), height)
    operands = [array for chunk in chunks for array in chunk]
    return pl.pallas_call(
        functools.partial(grad_kernel, len(chunks)),
        in_specs=[pl.BlockSpec(memory_space=pltpu.VMEM)] * len(operands),
        out_specs=[pl.BlockSpec(memory_space=pl.ANY)] * 2,
        out_shape=[jax.ShapeDtypeStruct((height, hidden), F32)] * 2,
        scratch_shapes=[
            pltpu.VMEM((tokens, height), BF16),
            pltpu.VMEM((tokens, hidden), BF16),
            pltpu.VMEM((2, tile, hidden), F32),
            pltpu.SemaphoreType.DMA((2,)),
        ],
        compiler_params=pltpu.CompilerParams(vmem_limit_bytes=10 * MIB),
        cost_estimate=pl.CostEstimate(flops=32 * tokens * height * hidden, bytes_accessed=0, transcendentals=0),
        name="weight_grads",
    )(*operands)


def swap(value, axis, bits):
    size = lax.axis_size(axis)
    return lax.ppermute(value, axis, [(i, i ^ bits) for i in range(size)])


def chip_sum(value, chips):
    value = value + swap(value, "tensor", 1)
    parts = [swap(value, "tensor", 2 * k) for k in range(1, chips)]
    return sum(parts, value)


def together(*values):
    return lax.optimization_barrier(values)


def spread(value, chips):
    offsets, blocks = [0], value[None]
    bit = chips // 2
    while bit > 1:
        offsets = offsets + [k ^ bit for k in offsets]
        blocks = jnp.concatenate([blocks, swap(blocks, "tensor", 2 * bit)])
        bit //= 2
    return (blocks, swap(blocks, "tensor", 2)), (offsets, [k ^ 1 for k in offsets])


def sum_over_chips(blocks):
    bit = 1
    while blocks.shape[1] > 1:
        sent = swap(blocks[:, 1::2].astype(BF16), "tensor", 2 * bit)
        blocks = blocks[:, 0::2] + sent.astype(F32)
        bit *= 2
    return blocks[:, 0]


def on_device(tokens, buckets, modulation, up_weight, down_weight, output_cotangent):
    rows, cols = tokens.shape
    chips = lax.axis_size("tensor") // 2
    groups = lax.axis_size("dp")
    width = cols * chips * 2
    height = width // groups
    blocked = cols % 128 == 0 and chips == groups
    place_in_tensor, group = lax.axis_index("tensor"), lax.axis_index("dp")
    chip, core = place_in_tensor // 2, place_in_tensor % 2
    spot = jnp.stack([chip, core, group]).astype(jnp.int32)
    order = chip ^ jnp.arange(chips)

    def with_sibling(arrays):
        other = [swap(array, "tensor", 1) for array in arrays]
        if blocked:
            blocks = lambda side: [
                (k, j, array) for ks, array in zip(offsets, side) for j, k in enumerate(ks)
            ]
            return Piece([blocks(arrays), blocks(other)])
        both = [jnp.concatenate(side) for side in (arrays, other)]
        pair = jnp.stack([jnp.where(core == 0, *both), jnp.where(core == 0, *both[::-1])], axis=1)
        pair = jnp.take(pair, jnp.argsort(jnp.array(sum(offsets, [])) ^ chip), axis=0)
        return Piece([[(0, 0, pair.transpose(2, 3, 0, 1, 4).reshape(1, 2, rows, width))]])

    x = tokens.astype(F32)
    cot = output_cotangent.astype(F32)
    cond = modulation.at[buckets].get(mode="promise_in_bounds")
    shift, scale, gate = cond[:, 0], cond[:, 1], cond[:, 2]
    dvel = (cot * gate).astype(BF16)
    sums = chip_sum(jnp.stack([jnp.sum(x, axis=1), jnp.sum(x * x, axis=1)]), chips)
    mean = sums[0] / width
    rstd = lax.rsqrt(sums[1] / width - mean * mean + 1e-06)[:, None]
    xhat = (x - mean[:, None]) * rstd
    h = (xhat * (1.0 + scale) + shift).astype(BF16)

    spot = bring(spot, up_weight, down_weight)
    value = jnp.stack([h, dvel])
    if chips == 4 and groups == 4 and blocked:
        along_z = lambda array, k: swap(array, "tensor", 2 * k)
        sibling = lambda array: swap(array, "tensor", 1)
        piece = lambda *sides: Piece([[(k, *block) for k, block in enumerate(side)] for side in sides])

        near0 = value[None]
        left0, right0 = swap(near0, "dp", 1), swap(near0, "dp", 2)
        near1, near2, left0, right0, corner0, near0_s, spot = together(
            along_z(near0, 1), along_z(near0, 2), left0, right0, swap(left0, "dp", 2), sibling(near0), spot
        )
        near3, left1, right1, near1_s, near2_s = together(
            along_z(near2, 1), swap(near1, "dp", 1), swap(near1, "dp", 2), sibling(near1), sibling(near2)
        )
        near23 = jnp.concatenate((near2, near3))
        near = piece(
            ((0, near0), (0, near1), (0, near2), (0, near3)),
            ((0, near0_s), (0, near1_s), (0, near2_s), (0, sibling(near3))),
        )
        own = chunk_products(spot, [near], up_weight, down_weight, height)
        keep_dh, give_dh = back(spot, own[0], up_weight, chips, 2, "dh_share")
        given_dh = sibling(give_dh)
        keep_vel, give_vel = back(spot, own[1], down_weight, chips, 2, "velocity_share")
        early = jnp.concatenate((left0, right0, left1, right1, corner0))
        own, keep_dh, given_dh, keep_vel, give_vel, early_s, left23, right23 = together(
            own, keep_dh, given_dh, keep_vel, give_vel, sibling(early), swap(near23, "dp", 1), swap(near23, "dp", 2)
        )
        given_vel, far23_s = together(sibling(give_vel), sibling(jnp.concatenate((left23, right23))))
        dh = keep_dh.astype(F32) + given_dh.astype(F32)
        half = rows // 2
        corner2, corner3 = (
            swap(jnp.concatenate((left23[:1], left1[:, :, :half]), axis=2), "dp", 2),
            swap(jnp.concatenate((right23[1:], right1[:, :, half:]), axis=2), "dp", 1),
        )
        velocity = keep_vel.astype(F32) + given_vel.astype(F32)
        half_dh, half_vel = along_z(dh[1::2].astype(BF16), 1), along_z(velocity[1::2].astype(BF16), 1)
        left = piece(
            ((0, left0), (0, left1), (0, left23), (1, left23)),
            ((0, early_s), (2, early_s), (0, far23_s), (1, far23_s)),
        )
        right = piece(
            ((0, right0), (0, right1), (0, right23), (1, right23)),
            ((1, early_s), (3, early_s), (2, far23_s), (3, far23_s)),
        )
        distant = chunk_products(spot, [left, right], up_weight, down_weight, height)
        distant, half_dh, corner2, corner3 = together(distant, half_dh, corner2, corner3)
        dh = dh[::2] + half_dh.astype(F32)
        got_dh = along_z(dh[1].astype(BF16), 2)
        distant, half_vel, corner2, corner3 = together(distant, half_vel, corner2, corner3)
        velocity = velocity[::2] + half_vel.astype(F32)
        sent_vel = velocity[1].astype(BF16)
        corner1 = jnp.concatenate((corner2[:, :, rows:], corner3[:, :, rows:]), axis=2)
        late = jnp.concatenate((corner1, corner2[:, :, :rows], corner3[:, :, :rows]))
        late_s = sibling(late)
        corner = piece(
            ((0, corner0), (0, late), (1, late), (2, late)),
            ((4, early_s), (0, late_s), (1, late_s), (2, late_s)),
        )
        last = chunk_products(spot, [corner], up_weight, down_weight, height, 0.02)
        last, got_dh, sent_vel = together(last, got_dh, sent_vel)
        dh = dh[0] + got_dh.astype(F32)
        dxhat = dh * (1.0 + scale)
        sums = jnp.stack([jnp.sum(dxhat, axis=1), jnp.sum(dxhat * xhat, axis=1)])
        sums, gate = together(sums, gate)
        sums = sums + sibling(sums)
        sums = (sums + along_z(sums, 1) + along_z(sums, 2) + along_z(sums, 3)) / width
        velocity = velocity[0] + along_z(sent_vel, 2).astype(F32)
        chunks = [own, distant, last]
    else:
        arrays, offsets = spread(value, chips)
        near = with_sibling(arrays)
        chunks = [chunk_products(spot, [near], up_weight, down_weight, height)]
        shares = [
            back(spot, chunks[0][j], weight, chips, len(near.sides), name)
            for j, weight, name in ((0, up_weight, "dh_share"), (1, down_weight, "velocity_share"))
        ]
        if blocked:
            keep, give = map(jnp.stack, zip(*shares))
        else:
            pair = jnp.concatenate([share[0] for share in shares])
            pair = jnp.take(pair.reshape(2, rows, chips, 2, cols).transpose(0, 2, 3, 1, 4), order, axis=1)
            keep = jnp.where(core == 0, pair[:, :, 0], pair[:, :, 1])
            give = jnp.where(core == 0, pair[:, :, 1], pair[:, :, 0])
        dh, velocity = sum_over_chips(keep.astype(F32) + swap(give, "tensor", 1).astype(F32))
        for m in range(1, groups):
            far = with_sibling([swap(array, "dp", m) for array in arrays])
            chunks.append(chunk_products(spot, [far], up_weight, down_weight, height))
        dxhat = dh * (1.0 + scale)
        sums = chip_sum(jnp.stack([jnp.sum(dxhat, axis=1), jnp.sum(dxhat * xhat, axis=1)]), chips) / width
    mixed = (x + gate * velocity).astype(BF16)
    token_grad = cot + rstd * (dxhat - sums[0][:, None] - xhat * sums[1][:, None])

    grad_up, grad_down = weight_grads(chunks)
    return mixed, token_grad.astype(BF16), grad_up, grad_down


def solution(mesh):
    rows, cols = P("dp", "tensor"), P(None, "tensor")
    return jax.shard_map(
        on_device,
        mesh=mesh,
        in_specs=(rows, P("dp"), P(None, None, "tensor"), cols, cols, rows),
        out_specs=(rows,) * 4,
        check_vma=False,
    )
```

```python
import functools
import math

import jax
import jax.numpy as jnp
from jax import lax
from jax.experimental import pallas as pl
from jax.experimental.pallas import tpu as pltpu
from jax.sharding import PartitionSpec as P

GELU_C = math.sqrt(2.0 / math.pi)
GELU_A = 0.044715
MIB = 1024 * 1024
F32 = jnp.float32
BF16 = jnp.bfloat16


def gelu_and_slope(v):
    square = v * v
    t = jnp.tanh(GELU_C * v * (1.0 + GELU_A * square))
    half = 0.5 * (1.0 + t)
    slope = half + (0.5 * GELU_C) * v * (1.0 - t * t) * (1.0 + (3.0 * GELU_A) * square)
    return v * half, slope


def each_column_tile(length, body, loop):
    tile = next((t for t in (256, 128) if length % t == 0), length)
    if not loop:
        for start in range(0, length, tile):
            body(slice(start, start + tile))
        return

    @pl.loop(0, length // tile)
    def _(i):
        body(pl.ds(pl.multiple_of(i * tile, 128), tile))


def call(kernel, name, operands, outs, scratch, flops, weight=8):
    return pl.pallas_call(
        kernel,
        in_specs=[pl.BlockSpec(memory_space=pltpu.SMEM)]
        + [pl.BlockSpec(memory_space=pltpu.VMEM)] * (len(operands) - 1),
        out_specs=[pl.BlockSpec(memory_space=pltpu.VMEM)] * len(outs),
        out_shape=outs,
        scratch_shapes=scratch,
        compiler_params=pltpu.CompilerParams(vmem_limit_bytes=12 * MIB),
        cost_estimate=pl.CostEstimate(flops=int(weight * flops), bytes_accessed=0, transcendentals=0),
        name=name,
    )(*operands)


class Piece:
    def __init__(self, sides):
        self.sides = sides

    def arrays(self):
        return [array for side in self.sides for _, _, array in side]

    def rows(self):
        return self.sides[0][0][2].shape[2]

    def bind(self, refs):
        refs = list(refs)
        return Piece([[(offset, index, refs.pop(0)) for offset, index, _ in side] for side in self.sides])


def bind_all(pieces, refs):
    bound = []
    for piece in pieces:
        count = len(piece.arrays())
        bound.append(piece.bind(refs[:count]))
        refs = refs[count:]
    return bound, refs


def place(dest, row, piece, which, spot):
    rows = piece.rows()
    for side, entries in enumerate(piece.sides):
        for offset, base, ref in entries:
            cols = ref.shape[3]
            if len(piece.sides) == 1:
                dest[row : row + rows, :] = ref[base, which]
            else:
                block = (spot[0] ^ offset) * 2 + (spot[1] ^ side)
                dest[row : row + rows, pl.ds(pl.multiple_of(block * cols, 128), cols)] = ref[base, which]


def hidden_tiles(h, dvel, up, down, act, dpre):
    def products(cols):
        value, slope = gelu_and_slope(jnp.dot(h[...], up[:, cols], preferred_element_type=F32))
        act[:, cols] = value.astype(BF16)
        dact = jnp.dot(dvel[...], down[:, cols], preferred_element_type=F32)
        dpre[:, cols] = (dact * slope).astype(BF16)

    each_column_tile(up.shape[1], products, loop=h.shape[0] > 256)


def bring_kernel(spot, up, down, out):
    for j in range(spot.shape[0]):
        out[j] = spot[j]


def bring(spot, up, down):
    return pl.pallas_call(
        bring_kernel,
        in_specs=[pl.BlockSpec(memory_space=pltpu.SMEM)] + [pl.BlockSpec(memory_space=pltpu.VMEM)] * 2,
        out_specs=pl.BlockSpec(memory_space=pltpu.SMEM),
        out_shape=jax.ShapeDtypeStruct(spot.shape, spot.dtype),
        compiler_params=pltpu.CompilerParams(vmem_limit_bytes=MIB),
        name="bring_weights",
    )(spot, up, down)


def tokens_kernel(pieces, spot, *refs):
    pieces, (up, down, dpre, act, h_cols, d_cols, h, dvel) = bind_all(pieces, refs)
    row = 0
    for piece in pieces:
        place(h, row, piece, 0, spot)
        place(dvel, row, piece, 1, spot)
        row += piece.rows()
    height = h_cols.shape[1]
    mine = pl.ds(pl.multiple_of(spot[2] * height, 128), height)
    h_cols[...] = h[:, mine]
    d_cols[...] = dvel[:, mine]
    hidden_tiles(h, dvel, up, down, act, dpre)


def chunk_products(spot, pieces, up, down, height, weight=8):
    width, hidden = up.shape
    rows = sum(piece.rows() for piece in pieces)
    return call(
        functools.partial(tokens_kernel, pieces),
        "chunk_products",
        [spot, *[array for piece in pieces for array in piece.arrays()], up, down],
        [jax.ShapeDtypeStruct((rows, hidden), BF16)] * 2 + [jax.ShapeDtypeStruct((rows, height), BF16)] * 2,
        [pltpu.VMEM((rows, width), BF16)] * 2,
        4 * rows * width * hidden,
        weight,
    )


def back_kernel(left_spot, left, weight, *parts):
    *parts, block = parts
    chips, _, cols = parts[0].shape
    wide = cols * len(parts)
    for k in range(chips):
        first = 0 if chips == 1 else pl.multiple_of((left_spot[0] ^ k) * wide, 128)
        block[...] = lax.dot_general(
            left[...], weight[pl.ds(first, wide), :], (((1,), (1,)), ((), ())), preferred_element_type=F32
        ).astype(BF16)
        for side, part in enumerate(parts):
            if len(parts) == 1:
                part[k] = block[...]
            else:
                part[k] = block[:, pl.ds(pl.multiple_of((left_spot[1] ^ side) * cols, 128), cols)]


def back(spot, left, weight, chips, sides, name):
    rows, hidden = left.shape
    width = weight.shape[0]
    if sides == 1:
        chips = 1
    cols = width // (chips * sides)
    return call(
        back_kernel,
        name,
        [spot, left, weight],
        [jax.ShapeDtypeStruct((chips, rows, cols), BF16)] * sides,
        [pltpu.VMEM((rows, cols * sides), BF16)],
        2 * rows * width * hidden,
    )


def grad_kernel(chunks, *refs):
    sources, (grad_up, grad_down, left, right, out, sems) = refs[: 4 * chunks], refs[4 * chunks :]
    copies = [None, None]
    turn = 0
    for grad, first in ((grad_down, 1), (grad_up, 0)):
        row = 0
        for j in range(chunks):
            some = slice(row, row + sources[4 * j].shape[0])
            right[some, :] = sources[4 * j + first][...]
            left[some, :] = sources[4 * j + 2 + first][...]
            row = some.stop
        tile = out.shape[1]
        for start in range(0, grad.shape[0], tile):
            slot = turn % 2
            if copies[slot] is not None:
                copies[slot].wait()
            some = slice(start, start + tile)

            out[slot] = lax.dot_general(
                left[:, some], right[...], (((0,), (0,)), ((), ())), preferred_element_type=F32
            )
            copies[slot] = pltpu.make_async_copy(out.at[slot], grad.at[some], sems.at[slot])
            copies[slot].start()
            turn += 1
    for copy in copies:
        if copy is not None:
            copy.wait()


def weight_grads(chunks):
    tokens = sum(chunk[0].shape[0] for chunk in chunks)
    hidden, height = chunks[0][0].shape[1], chunks[0][2].shape[1]
    tile = next((t for t in (384, 256, 128) if height % t == 0), height)
    operands = [array for chunk in chunks for array in chunk]
    return pl.pallas_call(
        functools.partial(grad_kernel, len(chunks)),
        in_specs=[pl.BlockSpec(memory_space=pltpu.VMEM)] * len(operands),
        out_specs=[pl.BlockSpec(memory_space=pl.ANY)] * 2,
        out_shape=[jax.ShapeDtypeStruct((height, hidden), F32)] * 2,
        scratch_shapes=[
            pltpu.VMEM((tokens, height), BF16),
            pltpu.VMEM((tokens, hidden), BF16),
            pltpu.VMEM((2, tile, hidden), F32),
            pltpu.SemaphoreType.DMA((2,)),
        ],
        compiler_params=pltpu.CompilerParams(vmem_limit_bytes=12 * MIB),
        cost_estimate=pl.CostEstimate(flops=32 * tokens * height * hidden, bytes_accessed=0, transcendentals=0),
        name="weight_grads",
    )(*operands)


def swap(value, axis, bits):
    size = lax.axis_size(axis)
    return lax.ppermute(value, axis, [(i, i ^ bits) for i in range(size)])


def chip_sum(value, chips):
    value = value + swap(value, "tensor", 1)
    parts = [swap(value, "tensor", 2 * k) for k in range(1, chips)]
    return sum(parts, value)


def together(*values):
    return lax.optimization_barrier(values)


def spread(value, chips):
    offsets, blocks = [0], value[None]
    bit = chips // 2
    while bit > 1:
        offsets = offsets + [k ^ bit for k in offsets]
        blocks = jnp.concatenate([blocks, swap(blocks, "tensor", 2 * bit)])
        bit //= 2
    return (blocks, swap(blocks, "tensor", 2)), (offsets, [k ^ 1 for k in offsets])


def sum_over_chips(blocks):
    bit = 1
    while blocks.shape[1] > 1:
        sent = swap(blocks[:, 1::2].astype(BF16), "tensor", 2 * bit)
        blocks = blocks[:, 0::2] + sent.astype(F32)
        bit *= 2
    return blocks[:, 0]


def on_device(tokens, buckets, modulation, up_weight, down_weight, output_cotangent):
    rows, cols = tokens.shape
    chips = lax.axis_size("tensor") // 2
    groups = lax.axis_size("dp")
    width = cols * chips * 2
    height = width // groups
    blocked = cols % 128 == 0 and chips == groups
    place_in_tensor, group = lax.axis_index("tensor"), lax.axis_index("dp")
    chip, core = place_in_tensor // 2, place_in_tensor % 2
    spot = jnp.stack([chip, core, group]).astype(jnp.int32)
    order = chip ^ jnp.arange(chips)

    def with_sibling(arrays):
        other = [swap(array, "tensor", 1) for array in arrays]
        if blocked:
            blocks = lambda side: [
                (k, j, array) for ks, array in zip(offsets, side) for j, k in enumerate(ks)
            ]
            return Piece([blocks(arrays), blocks(other)])
        both = [jnp.concatenate(side) for side in (arrays, other)]
        pair = jnp.stack([jnp.where(core == 0, *both), jnp.where(core == 0, *both[::-1])], axis=1)
        pair = jnp.take(pair, jnp.argsort(jnp.array(sum(offsets, [])) ^ chip), axis=0)
        return Piece([[(0, 0, pair.transpose(2, 3, 0, 1, 4).reshape(1, 2, rows, width))]])

    x = tokens.astype(F32)
    cot = output_cotangent.astype(F32)
    cond = modulation.at[buckets].get(mode="promise_in_bounds")
    shift, scale, gate = cond[:, 0], cond[:, 1], cond[:, 2]
    dvel = (cot * gate).astype(BF16)
    sums = chip_sum(jnp.stack([jnp.sum(x, axis=1), jnp.sum(x * x, axis=1)]), chips)
    mean = sums[0] / width
    rstd = lax.rsqrt(sums[1] / width - mean * mean + 1e-06)[:, None]
    xhat = (x - mean[:, None]) * rstd
    h = (xhat * (1.0 + scale) + shift).astype(BF16)

    spot = bring(spot, up_weight, down_weight)
    value = jnp.stack([h, dvel])
    if chips == 4 and groups == 4 and blocked:
        along_z = lambda array, k: swap(array, "tensor", 2 * k)
        sibling = lambda array: swap(array, "tensor", 1)
        piece = lambda *sides: Piece([[(k, *block) for k, block in enumerate(side)] for side in sides])

        near0 = value[None]
        left0, right0 = swap(near0, "dp", 1), swap(near0, "dp", 2)
        near1, near2, left0, right0, corner0, near0_s, spot = together(
            along_z(near0, 1), along_z(near0, 2), left0, right0, swap(left0, "dp", 2), sibling(near0), spot
        )
        near3, left1, right1, near1_s, near2_s = together(
            along_z(near2, 1), swap(near1, "dp", 1), swap(near1, "dp", 2), sibling(near1), sibling(near2)
        )
        near23 = jnp.concatenate((near2, near3))
        near = piece(
            ((0, near0), (0, near1), (0, near2), (0, near3)),
            ((0, near0_s), (0, near1_s), (0, near2_s), (0, sibling(near3))),
        )
        own = chunk_products(spot, [near], up_weight, down_weight, height)
        keep_dh, give_dh = back(spot, own[0], up_weight, chips, 2, "dh_share")
        given_dh = sibling(give_dh)
        keep_vel, give_vel = back(spot, own[1], down_weight, chips, 2, "velocity_share")
        early = jnp.concatenate((left0, right0, left1, right1, corner0))
        own, keep_dh, given_dh, keep_vel, give_vel, early_s, left23, right23 = together(
            own, keep_dh, given_dh, keep_vel, give_vel, sibling(early), swap(near23, "dp", 1), swap(near23, "dp", 2)
        )
        given_vel, far23_s = together(sibling(give_vel), sibling(jnp.concatenate((left23, right23))))
        dh = keep_dh.astype(F32) + given_dh.astype(F32)
        half = rows // 2
        corner2, corner3 = (
            swap(jnp.concatenate((left23[:1], left1[:, :, :half]), axis=2), "dp", 2),
            swap(jnp.concatenate((right23[1:], right1[:, :, half:]), axis=2), "dp", 1),
        )
        velocity = keep_vel.astype(F32) + given_vel.astype(F32)
        half_dh, half_vel = along_z(dh[1::2].astype(BF16), 1), along_z(velocity[1::2].astype(BF16), 1)
        left = piece(
            ((0, left0), (0, left1), (0, left23), (1, left23)),
            ((0, early_s), (2, early_s), (0, far23_s), (1, far23_s)),
        )
        right = piece(
            ((0, right0), (0, right1), (0, right23), (1, right23)),
            ((1, early_s), (3, early_s), (2, far23_s), (3, far23_s)),
        )
        distant = chunk_products(spot, [left, right], up_weight, down_weight, height)
        distant, half_dh, half_vel, corner2, corner3 = together(distant, half_dh, half_vel, corner2, corner3)
        dh, velocity = dh[::2] + half_dh.astype(F32), velocity[::2] + half_vel.astype(F32)
        got_dh = along_z(dh[1].astype(BF16), 2)
        sent_vel = velocity[1].astype(BF16)
        corner1 = jnp.concatenate((corner2[:, :, rows:], corner3[:, :, rows:]), axis=2)
        late = jnp.concatenate((corner1, corner2[:, :, :rows], corner3[:, :, :rows]))
        late_s = sibling(late)
        corner = piece(
            ((0, corner0), (0, late), (1, late), (2, late)),
            ((4, early_s), (0, late_s), (1, late_s), (2, late_s)),
        )
        last = chunk_products(spot, [corner], up_weight, down_weight, height)
        last, got_dh, sent_vel = together(last, got_dh, sent_vel)
        dh = dh[0] + got_dh.astype(F32)
        dxhat = dh * (1.0 + scale)
        sums = jnp.stack([jnp.sum(dxhat, axis=1), jnp.sum(dxhat * xhat, axis=1)])
        sums, gate = together(sums, gate)
        sums = sums + sibling(sums)
        sums = (sums + along_z(sums, 1) + along_z(sums, 2) + along_z(sums, 3)) / width
        velocity = velocity[0] + along_z(sent_vel, 2).astype(F32)
        chunks = [own, distant, last]
    else:
        arrays, offsets = spread(value, chips)
        near = with_sibling(arrays)
        chunks = [chunk_products(spot, [near], up_weight, down_weight, height)]
        shares = [
            back(spot, chunks[0][j], weight, chips, len(near.sides), name)
            for j, weight, name in ((0, up_weight, "dh_share"), (1, down_weight, "velocity_share"))
        ]
        if blocked:
            keep, give = map(jnp.stack, zip(*shares))
        else:
            pair = jnp.concatenate([share[0] for share in shares])
            pair = jnp.take(pair.reshape(2, rows, chips, 2, cols).transpose(0, 2, 3, 1, 4), order, axis=1)
            keep = jnp.where(core == 0, pair[:, :, 0], pair[:, :, 1])
            give = jnp.where(core == 0, pair[:, :, 1], pair[:, :, 0])
        dh, velocity = sum_over_chips(keep.astype(F32) + swap(give, "tensor", 1).astype(F32))
        for m in range(1, groups):
            far = with_sibling([swap(array, "dp", m) for array in arrays])
            chunks.append(chunk_products(spot, [far], up_weight, down_weight, height))
        dxhat = dh * (1.0 + scale)
        sums = chip_sum(jnp.stack([jnp.sum(dxhat, axis=1), jnp.sum(dxhat * xhat, axis=1)]), chips) / width
    mixed = (x + gate * velocity).astype(BF16)
    token_grad = cot + rstd * (dxhat - sums[0][:, None] - xhat * sums[1][:, None])

    grad_up, grad_down = weight_grads(chunks)
    return mixed, token_grad.astype(BF16), grad_up, grad_down


def solution(mesh):
    rows, cols = P("dp", "tensor"), P(None, "tensor")
    return jax.shard_map(
        on_device,
        mesh=mesh,
        in_specs=(rows, P("dp"), P(None, None, "tensor"), cols, cols, rows),
        out_specs=(rows,) * 4,
        check_vma=False,
    )
```
